512 devices in a mesh: dp: 4 (over x_hi, core), expert: 128 (over y, z, x_lo).
Axes of the slice: x: 4 (x_hi: 2, x_lo: 2; x = x_hi * 2 + x_lo), y: 4, z: 16, core: 2. Of those that a mesh axis runs over, the one named last changes fastest.
Arguments:
- gradient: bfloat16 [4, 64, 2048, 768], P('dp', None, 'expert'), may hold values from -6 to 6
- momentum: float32 [64, 2048, 768], P('dp', 'expert'), may hold values from -31 to 31
Outputs:
- new_momentum: float32 [64, 2048, 768], P('dp', 'expert')
- update: float32 [64, 2048, 768], P('dp', 'expert')
The draws below stay inside these ranges and needn't reach their ends.
All inputs are finite; a program needn't handle non-finite values.
Results may differ from the reference program's by a relative error of at most 0.0003.
Values sent between devices are 32-bit elements; how exact they have to be, the bound alone decides.
A program may use at most 64 MiB of HBM per device.

```python
import math
import jax
import jax.numpy as jnp
from jax import lax

D = 2048
FF = 768
ITERS = 2
EXPERTS = 64
N_DP = 4


def draw_momentum(key, part):
    key = jax.random.fold_in(key, 7)
    subkeys = jax.random.split(key, 3)
    lower_log = math.log(0.3)
    upper_log = math.log(3.0)
    row_scale = jnp.exp(jax.random.uniform(subkeys[0], (EXPERTS, D, 1), jnp.float32, lower_log, upper_log))
    rising = 1.0 + 2.0 * jnp.arange(D, dtype=jnp.float32).reshape(1, D, 1) / (D - 1)
    col_scale = jnp.exp(jax.random.uniform(subkeys[1], (EXPERTS, 1, FF), jnp.float32, lower_log, upper_log))
    entries = jnp.clip(jax.random.normal(subkeys[2], (EXPERTS, D, FF), jnp.float32), -4.0, 4.0)
    return 0.25 * entries * row_scale * rising * col_scale


def raised(values, key, source, target, parts, factor):
    owner, partner = [(jnp.arange(values.shape[position]) // (values.shape[position] // parts)).reshape([-1 if axis == position else 1 for axis in range(values.ndim)]) for position in (source, target)]
    chosen = jax.random.permutation(key, parts)[partner]
    strong = (owner == chosen) | (owner == (partner + parts // 2) % parts)
    return jnp.where(strong, factor * values, values)


def block_levels(own_key, dims, cuts, low, top_value):
    loudness, own = 1.0, jax.random.fold_in(own_key, 6)
    for position, parts in cuts:
        steps = jnp.exp(jax.random.uniform(jax.random.fold_in(own, position), (parts,), jnp.float32, low / len(cuts), top_value / len(cuts)))
        loudness = loudness * jnp.repeat(steps, dims[position] // parts).reshape([-1 if axis == position else 1 for axis in range(len(dims))])
    return loudness


def noise_with(key, shape, width, limit, cuts, heavy, kind=jnp.bfloat16):
    values = width * jax.random.normal(key, shape, jnp.float32)
    if cuts:
        values = values * block_levels(key, shape, cuts, -0.22, 0.18)
    return jnp.clip(raised(values, jax.random.fold_in(key, 3), *heavy), -limit, limit).astype(kind)


def setup_inputs(seed: int = 0) -> dict:
    streams_of = jax.random.split(jax.random.key(seed), 3)
    return {
        "gradient": noise_with(streams_of[0], (N_DP, EXPERTS, D, FF), 1.0, 6.0, ((0, 4), (2, 128)), (0, 1, 4, 2.0)),
        "momentum": draw_momentum(jax.random.fold_in(streams_of[2], 71), 0),
    }


first_coeff = 3.4445
second_coeff = -4.775
third_coeff = 2.0315
momentum_keep = 0.95
norm_epsilon = 1e-07

def orthogonalize(matrix):
    square_sum = jnp.sum(matrix * matrix)
    iterate = matrix
    for repeat_index in range(ITERS):
        if repeat_index == 0:
            factor = 1.0 / (jnp.sqrt(square_sum) + norm_epsilon)
        else:
            factor = 1.0
        gram = jnp.dot(iterate.T, iterate, precision=lax.Precision.HIGHEST, preferred_element_type=jnp.float32)
        scaled = gram * (factor * factor)
        polynomial = second_coeff * scaled + third_coeff * jnp.dot(scaled, scaled, precision=lax.Precision.HIGHEST, preferred_element_type=jnp.float32)
        iterate = factor * (first_coeff * iterate + jnp.dot(iterate, polynomial, precision=lax.Precision.HIGHEST, preferred_element_type=jnp.float32))
    return D ** 0.5 * iterate

def reference(gradient, momentum):
    grad_sum = gradient[0].astype(jnp.float32)
    for replica in range(1, N_DP):
        grad_sum = grad_sum + gradient[replica].astype(jnp.float32)
    new_momentum = momentum_keep * momentum + grad_sum
    update = lax.map(orthogonalize, new_momentum)
    return (new_momentum, update)
```

```python
import jax
import jax.numpy as jnp
from jax import lax
from jax.experimental import pallas as pl
from jax.experimental.pallas import tpu as pltpu
from jax.sharding import PartitionSpec as P

D = 2048
FF = 768

first_coeff = 3.4445
second_coeff = -4.775
third_coeff = 2.0315
momentum_keep = 0.95
norm_epsilon = 1e-07

NY, NZ = 4, 16
EXP = 16
ROWS = 16
WAVES = 4
PER = EXP // WAVES
BLK = 256
PAIRS = ((0, 0), (0, 1), (0, 2), (1, 1), (1, 2), (2, 2))
DIAGONAL = (0, 3, 5)
HALF = 3 * BLK
PIECE = HALF // NY

MESH = pl.DeviceIdType.MESH
f32 = jnp.float32
bf16 = jnp.bfloat16


def split(value):
    high = value.astype(bf16)
    return high, (value - high.astype(f32)).astype(bf16)


def dot(left, right):
    return jnp.dot(left, right, preferred_element_type=f32)


def dot_rows(left, right):
    return lax.dot_general(left, right, (((0,), (0,)), ((), ())), preferred_element_type=f32)


def kernel(
    grad,
    mom,
    new_mom,
    upd,
    core_out,
    core_in,
    x_out,
    x_in,
    rows,
    gram,
    gram_core,
    half,
    gram_y,
    full,
    s_hi,
    s_lo,
    q_hi,
    q_lo,
    result,
    core_ss,
    core_rs,
    x_ss,
    x_rs,
    fwd_ss,
    fwd_rs,
    ret_ss,
    ret_rs,
    gc_ss,
    gc_rs,
    gy_ss,
    gy_rs,
    ay_ss,
    ay_rs,
    ac_ss,
    ac_rs,
):
    dp = lax.axis_index("dp")
    ex = lax.axis_index("expert")
    h, c = dp // 2, dp % 2
    y, z, a = ex // 32, (ex // 2) % NZ, ex % 2

    other_core = (h * 2 + 1 - c, ex)
    x_partner = ((1 - h) * 2 + c, ex)

    def z_peer(i):
        return (h * 2 + a, y * 32 + i * 2 + c)

    def y_peer(k):
        return (dp, ((y + k) % NY) * 32 + z * 2 + a)

    def remote(src, dst, ss, rs, to):
        return pltpu.make_async_remote_copy(
            src_ref=src, dst_ref=dst, send_sem=ss, recv_sem=rs, device_id=to, device_id_type=MESH
        )

    straight = a == c

    barrier = pltpu.get_barrier_semaphore()

    def greet(to):
        pl.semaphore_signal(barrier, inc=1, device_id=to, device_id_type=MESH)

    greet(other_core)
    greet(x_partner)
    for k in range(1, NY):
        greet(y_peer(k))
    for i in range(NZ):

        @pl.when(jnp.logical_not(jnp.logical_and(straight, z == i)))
        def _():
            greet(z_peer(i))

    pl.semaphore_wait(barrier, 5 + NZ - straight.astype(jnp.int32))

    def core_copy(side, w):
        return remote(core_out.at[side, w], core_in.at[side, w], core_ss.at[side, w], core_rs.at[side, w], other_core)

    def x_copy(w):
        return remote(x_out.at[w], x_in.at[w], x_ss.at[w], x_rs.at[w], x_partner)

    def base(side, core):
        owner_h = 1 - h if side == 0 else h
        return (owner_h * 2 + core) * EXP

    for w in range(WAVES):
        for side in range(2):
            for j in range(PER):
                core_out[side, w, j] = grad[0, base(side, 1 - c) + WAVES * j + w].astype(f32)
            core_copy(side, w).start()
    for w in range(WAVES):
        core_copy(0, w).wait_recv()
        for j in range(PER):
            x_out[w, j] = grad[0, base(0, c) + WAVES * j + w].astype(f32) + core_in[0, w, j]
        x_copy(w).start()
    for w in range(WAVES):
        core_copy(1, w).wait_recv()
        for j in range(PER):
            i = WAVES * j + w
            new_mom[i] = momentum_keep * mom[i] + (grad[0, base(1, c) + i].astype(f32) + core_in[1, w, j])

    def fwd_copy(i, slot):
        return remote(new_mom.at[i], rows.at[slot], fwd_ss.at[i], fwd_rs.at[slot], z_peer(i))

    for w in range(WAVES):
        x_copy(w).wait_recv()
        for j in range(PER):
            i = WAVES * j + w
            new_mom[i] = new_mom[i] + x_in[w, j]
            here = jnp.logical_and(straight, z == i)

            @pl.when(here)
            def _():
                rows[i] = new_mom[i]

            @pl.when(jnp.logical_not(here))
            def _():
                fwd_copy(i, z).start()

    for s in range(NZ):

        @pl.when(jnp.logical_not(jnp.logical_and(straight, z == s)))
        def _():
            fwd_copy(s, s).wait_recv()

    x0 = rows[...].reshape(NZ * ROWS, FF)
    x_hi, x_lo = split(x0)
    for b, (p, q) in enumerate(PAIRS):
        ph, plo = x_hi[:, p * BLK : (p + 1) * BLK], x_lo[:, p * BLK : (p + 1) * BLK]
        qh, qlo = x_hi[:, q * BLK : (q + 1) * BLK], x_lo[:, q * BLK : (q + 1) * BLK]
        gram[b] = dot_rows(ph, qh) + (dot_rows(ph, qlo) + dot_rows(plo, qh))

    gc = remote(gram.at[pl.ds(3 * (1 - c), 3)], gram_core, gc_ss, gc_rs, other_core)
    gc.start()
    gc.wait_recv()
    for k in range(3):
        half[pl.ds(k * BLK, BLK)] = gram[3 * c + k] + gram_core[k]

    def piece(p):
        return pl.ds(pl.multiple_of(p * PIECE, PIECE), PIECE)

    def gy_copy(k):
        return remote(half.at[piece((y + k) % NY)], gram_y.at[k - 1], gy_ss.at[k - 1], gy_rs.at[k - 1], y_peer(k))

    for k in range(1, NY):
        gy_copy(k).start()
    for k in range(1, NY):
        gy_copy(k).wait_recv()
    own = piece(y)
    full[c, own] = (half[own] + gram_y[0]) + (gram_y[1] + gram_y[2])

    def ay_copy(k, p):
        return remote(full.at[c, piece(p)], full.at[c, piece(p)], ay_ss.at[k - 1], ay_rs.at[k - 1], y_peer(k))

    def ac_copy(k, core):
        p = piece((y + NY - k) % NY)
        return remote(full.at[core, p], full.at[core, p], ac_ss.at[k], ac_rs.at[k], other_core)

    for k in range(1, NY):
        ay_copy(k, y).start()
    ac_copy(0, c).start()
    for k in range(1, NY):
        ay_copy(k, (y + NY - k) % NY).wait_recv()
        ac_copy(k, c).start()
    for k in range(NY):
        ac_copy(k, 1 - c).wait_recv()

    def block(b):
        return full[b // 3, (b % 3) * BLK : (b % 3 + 1) * BLK, :]

    eye = lax.broadcasted_iota(jnp.int32, (BLK, BLK), 0) == lax.broadcasted_iota(jnp.int32, (BLK, BLK), 1)
    on_diagonal = jnp.where(eye, block(0) + block(3) + block(5), 0.0)
    square_sum = jnp.sum(jnp.sum(on_diagonal, axis=1, keepdims=True), axis=0, keepdims=True)
    factor = 1.0 / (jnp.sqrt(square_sum) + norm_epsilon)
    scale = factor * factor

    def put(hi, lo, p, q, value):
        vh, vl = split(value)
        hi[p * BLK : (p + 1) * BLK, q * BLK : (q + 1) * BLK] = vh
        lo[p * BLK : (p + 1) * BLK, q * BLK : (q + 1) * BLK] = vl

    for b, (p, q) in enumerate(PAIRS):
        value = block(b) * scale
        put(s_hi, s_lo, p, q, value)
        if p != q:
            put(s_hi, s_lo, q, p, value.T)
    for b, (p, q) in enumerate(PAIRS):
        lh, ll = s_hi[p * BLK : (p + 1) * BLK, :], s_lo[p * BLK : (p + 1) * BLK, :]
        rh, rl = s_hi[:, q * BLK : (q + 1) * BLK], s_lo[:, q * BLK : (q + 1) * BLK]
        square = dot(lh, rh) + (dot(lh, rl) + dot(ll, rh))
        value = (second_coeff * scale) * block(b) + third_coeff * square
        if p == q:
            value = value + jnp.where(eye, first_coeff, 0.0)
        put(q_hi, q_lo, p, q, value)
        if p != q:
            put(q_hi, q_lo, q, p, value.T)

    def times(value, hi, lo):
        vh, vl = split(value)
        return dot(vh, hi[...]) + (dot(vh, lo[...]) + dot(vl, hi[...]))

    x1 = times(x0, q_hi, q_lo) * factor
    t1 = times(times(times(x1, q_hi, q_lo), s_hi, s_lo), q_hi, q_lo)
    t2 = times(times(times(t1, q_hi, q_lo), s_hi, s_lo), q_hi, q_lo)
    final = D**0.5 * (first_coeff * x1 + second_coeff * t1 + third_coeff * t2)
    result[...] = final.reshape(NZ, ROWS, FF)

    def ret_copy(s, slot):
        return remote(result.at[s], upd.at[slot], ret_ss.at[s], ret_rs.at[slot], z_peer(s))

    for s in range(NZ):
        here = jnp.logical_and(straight, z == s)

        @pl.when(here)
        def _():
            upd[s] = result[s]

        @pl.when(jnp.logical_not(here))
        def _():
            ret_copy(s, z).start()

    for w in range(WAVES):
        for side in range(2):
            core_copy(side, w).wait_send()
        x_copy(w).wait_send()
    gc.wait_send()
    for k in range(1, NY):
        gy_copy(k).wait_send()
        ay_copy(k, y).wait_send()
    for k in range(NY):
        ac_copy(k, c).wait_send()
    for s in range(NZ):

        @pl.when(jnp.logical_not(jnp.logical_and(straight, z == s)))
        def _():
            fwd_copy(s, s).wait_send()
            ret_copy(s, s).wait_send()
            ret_copy(s, s).wait_recv()


def shards(gradient, momentum):
    vmem = pl.BlockSpec(memory_space=pltpu.VMEM)
    dma = pltpu.SemaphoreType.DMA
    shape = jax.ShapeDtypeStruct(momentum.shape, f32)
    return pl.pallas_call(
        kernel,
        out_shape=(shape, shape),
        in_specs=[vmem, vmem],
        out_specs=(vmem, vmem),
        scratch_shapes=[
            pltpu.VMEM((2, WAVES, PER, ROWS, FF), f32),
            pltpu.VMEM((2, WAVES, PER, ROWS, FF), f32),
            pltpu.VMEM((WAVES, PER, ROWS, FF), f32),
            pltpu.VMEM((WAVES, PER, ROWS, FF), f32),
            pltpu.VMEM((NZ, ROWS, FF), f32),
            pltpu.VMEM((6, BLK, BLK), f32),
            pltpu.VMEM((3, BLK, BLK), f32),
            pltpu.VMEM((HALF, BLK), f32),
            pltpu.VMEM((NY - 1, PIECE, BLK), f32),
            pltpu.VMEM((2, HALF, BLK), f32),
            pltpu.VMEM((FF, FF), bf16),
            pltpu.VMEM((FF, FF), bf16),
            pltpu.VMEM((FF, FF), bf16),
            pltpu.VMEM((FF, FF), bf16),
            pltpu.VMEM((NZ, ROWS, FF), f32),
            dma((2, WAVES)),
            dma((2, WAVES)),
            dma((WAVES,)),
            dma((WAVES,)),
            dma((NZ,)),
            dma((NZ,)),
            dma((NZ,)),
            dma((NZ,)),
            dma,
            dma,
            dma((NY - 1,)),
            dma((NY - 1,)),
            dma((NY - 1,)),
            dma((NY - 1,)),
            dma((NY,)),
            dma((NY,)),
        ],
        compiler_params=pltpu.CompilerParams(
            collective_id=0, has_side_effects=True, vmem_limit_bytes=48 * 2**20
        ),
        name="muon",
    )(gradient, momentum)


def solution(mesh):
    placed = (P("dp", None, "expert", None), P("dp", "expert", None))
    return jax.shard_map(
        shards,
        mesh=mesh,
        in_specs=placed,
        out_specs=(P("dp", "expert", None), P("dp", "expert", None)),
        check_vma=False,
    )
```

```python
import functools

import jax
import jax.numpy as jnp
from jax import lax
from jax.experimental import pallas as pl
from jax.experimental.pallas import tpu as pltpu
from jax.sharding import PartitionSpec as P

D = 2048
FF = 768

first_coeff = 3.4445
second_coeff = -4.775
third_coeff = 2.0315
momentum_keep = 0.95
norm_epsilon = 1e-07

NY, NZ = 4, 16
EXP = 16
ROWS = 16
WAVES = 4
PER = EXP // WAVES
BLK = 256
PAIRS = ((0, 0), (0, 1), (0, 2), (1, 1), (1, 2), (2, 2))
DIAGONAL = (0, 3, 5)
HALF = 3 * BLK
PIECE = HALF // NY
HALF_PIECE = PIECE // 2

XAHEAD = 2
MESH = pl.DeviceIdType.MESH
f32 = jnp.float32
bf16 = jnp.bfloat16


def split(value):
    high = value.astype(bf16)
    return high, (value - high.astype(f32)).astype(bf16)


def dot(left, right):
    return jnp.dot(left, right, preferred_element_type=f32)


def dot_rows(left, right):
    return lax.dot_general(left, right, (((0,), (0,)), ((), ())), preferred_element_type=f32)


def kernel(
    grad_hbm,
    mom_hbm,
    new_mom,
    upd,
    grad,
    mom,
    core_out,
    core_in,
    x_out,
    x_in,
    rows,
    gram,
    gram_core,
    half,
    ry_in,
    ry_out,
    full,
    s_stack,
    q_stack,
    r_stack,
    t_stack,
    result,
    core_ss,
    core_rs,
    x_ss,
    x_rs,
    fwd_ss,
    fwd_rs,
    ret_ss,
    ret_rs,
    gc_ss,
    gc_rs,
    ry_ss,
    ry_rs,
    ay_ss,
    ay_rs,
    ac_ss,
    ac_rs,
    load_s,
    entered,
):
    dp = lax.axis_index("dp")
    ex = lax.axis_index("expert")
    h, c = dp // 2, dp % 2
    y, z, a = ex // 32, (ex // 2) % NZ, ex % 2

    other_core = (h * 2 + 1 - c, ex)
    x_partner = ((1 - h) * 2 + c, ex)

    def z_peer(i):
        return (h * 2 + a, y * 32 + i * 2 + c)

    def along_z(d):
        return (dp, y * 32 + ((z + d) % NZ) * 2 + a)

    def y_peer(k):
        return (dp, ((y + k) % NY) * 32 + z * 2 + a)

    def remote(src, dst, ss, rs, to):
        return pltpu.make_async_remote_copy(
            src_ref=src, dst_ref=dst, send_sem=ss, recv_sem=rs, device_id=to, device_id_type=MESH
        )

    straight = a == c

    loads = [
        pltpu.make_async_copy(grad_hbm, grad, load_s.at[0]),
        pltpu.make_async_copy(mom_hbm, mom, load_s.at[1]),
    ]
    for load in loads:
        load.start()

    pending = []

    def finish():
        for wait in pending:
            wait()

    def unless_here(s, then):
        pl.when(jnp.logical_not(jnp.logical_and(straight, z == s)))(then)

    barrier = pltpu.get_barrier_semaphore()

    def greet(to):
        pl.semaphore_signal(barrier, inc=1, device_id=to, device_id_type=MESH)

    greet(other_core)
    greet(x_partner)
    for k in range(1, NY):
        greet(y_peer(k))
    for d in (1, NZ - 1):
        greet(along_z(d))

    @pl.when(jnp.logical_not(straight))
    def _():
        for d in (0, 1, NZ - 1):
            greet(z_peer((z + d) % NZ))

    pl.semaphore_wait(barrier, 10 - 3 * straight.astype(jnp.int32))

    def hand_on(step):
        d = 2**step
        for away in (d, NZ - d):
            pl.semaphore_signal(entered.at[step], inc=1, device_id=along_z(away), device_id_type=MESH)
        pl.semaphore_wait(entered.at[step], 2)

    for load in loads:
        load.wait()

    def core_copy(side, w):
        return remote(core_out.at[side, w], core_in.at[side, w], core_ss.at[side, w], core_rs.at[side, w], other_core)

    def x_copy(w):
        return remote(x_out.at[w], x_in.at[w], x_ss.at[w], x_rs.at[w], x_partner)

    def base(side, core):
        owner_h = 1 - h if side == 0 else h
        return (owner_h * 2 + core) * EXP

    for side in range(2):
        for w in range(WAVES):
            for j in range(PER):
                core_out[side, w, j] = grad[0, base(side, 1 - c) + WAVES * j + w].astype(f32)
            core_copy(side, w).start()
            pending.append(core_copy(side, w).wait_send)

    def x_send(w):
        core_copy(0, w).wait_recv()
        for j in range(PER):
            x_out[w, j] = grad[0, base(0, c) + WAVES * j + w].astype(f32) + core_in[0, w, j]
        x_copy(w).start()
        pending.append(x_copy(w).wait_send)

    hand_on(0)
    for w in range(XAHEAD):
        x_send(w)
    hand_on(1)
    hand_on(2)

    def fwd_copy(i, slot):
        return remote(new_mom.at[i], rows.at[slot], fwd_ss.at[i], fwd_rs.at[slot], z_peer(i))

    for w in range(WAVES):
        core_copy(1, w).wait_recv()
        for j in range(PER):
            i = WAVES * j + w
            new_mom[i] = momentum_keep * mom[i] + (grad[0, base(1, c) + i].astype(f32) + core_in[1, w, j])
        x_copy(w).wait_recv()
        if w + XAHEAD < WAVES:
            x_send(w + XAHEAD)
        for j in range(PER):
            i = WAVES * j + w
            new_mom[i] = new_mom[i] + x_in[w, j]
        if w >= 1:

            @pl.when(z % WAVES >= w)
            def _():
                for j in range(PER):
                    i = WAVES * j + w - 1
                    unless_here(i, fwd_copy(i, i).wait_send)

        for j in range(PER):
            i = WAVES * j + w
            @pl.when(jnp.logical_and(straight, z == i))
            def _():
                rows[i] = new_mom[i]

            unless_here(i, fwd_copy(i, z).start)

    def fwd_finish():
        for w in range(WAVES):

            def left():
                for j in range(PER):
                    i = WAVES * j + w
                    unless_here(i, fwd_copy(i, i).wait_send)

            if w + 1 < WAVES:
                pl.when(z % WAVES < w + 1)(left)
            else:
                left()

    pending.append(fwd_finish)

    for s in range(NZ):

        @pl.when(jnp.logical_not(jnp.logical_and(straight, z == s)))
        def _():
            fwd_copy(s, s).wait_recv()

    x0 = rows[...].reshape(NZ * ROWS, FF)
    x_hi, x_lo = split(x0)
    left = jnp.concatenate([x_hi, x_hi, x_lo], axis=0)
    right = jnp.concatenate([x_hi, x_lo, x_hi], axis=0)
    for b, (p, q) in enumerate(PAIRS):
        gram[b] = dot_rows(left[:, p * BLK : (p + 1) * BLK], right[:, q * BLK : (q + 1) * BLK])

    gc = remote(gram.at[pl.ds(3 * (1 - c), 3)], gram_core, gc_ss, gc_rs, other_core)
    gc.start()
    pending.append(gc.wait_send)
    gc.wait_recv()
    for k in range(3):
        half[pl.ds(k * BLK, BLK)] = gram[3 * c + k] + gram_core[k]

    up, down = y_peer(1), y_peer(NY - 1)
    p_up, p_far, p_down = (y + 1) % NY, (y + 2) % NY, (y + NY - 1) % NY

    def part(p, side):
        return pl.ds(pl.multiple_of(p * PIECE + side * HALF_PIECE, HALF_PIECE), HALF_PIECE)

    def ry_copy(k, src, to):
        return remote(src, ry_in.at[k], ry_ss.at[k], ry_rs.at[k], to)

    ry = [
        ry_copy(0, half.at[part(p_far, 0)], up),
        ry_copy(1, half.at[part(p_far, 1)], down),
        ry_copy(2, half.at[part(p_up, 1)], up),
        ry_copy(3, half.at[part(p_down, 0)], down),
        ry_copy(4, ry_out.at[0], up),
        ry_copy(5, ry_out.at[1], down),
    ]
    for k in range(4):
        ry[k].start()
    for k, p in ((0, p_up), (1, p_down)):
        ry[k].wait_recv()
        ry_out[k] = ry_in[k] + half[part(p, k)]
        ry[4 + k].start()
    for k in range(2, 6):
        ry[k].wait_recv()
    full[c, part(y, 0)] = half[part(y, 0)] + (ry_in[3] + ry_in[4])
    full[c, part(y, 1)] = half[part(y, 1)] + (ry_in[2] + ry_in[5])
    for copy in ry:
        pending.append(copy.wait_send)

    def ay_copy(k, p, side, to):
        place = full.at[c, part(p, side)]
        return remote(place, place, ay_ss.at[k], ay_rs.at[k], to)

    arrivals = ((p_down, 0), (p_up, 1), (p_down, 1), (p_up, 0), (p_far, 0), (p_far, 1))

    def ac_copy(k, core):
        place = full.at[core, part(*arrivals[k])]
        return remote(place, place, ac_ss.at[k], ac_rs.at[k], other_core)

    def own_copy(core):
        place = full.at[core, pl.ds(pl.multiple_of(y * PIECE, PIECE), PIECE)]
        return remote(place, place, ac_ss.at[6], ac_rs.at[6], other_core)

    ay = [
        ay_copy(0, y, 0, up),
        ay_copy(1, y, 1, down),
        ay_copy(2, y, 1, up),
        ay_copy(3, y, 0, down),
        ay_copy(4, p_down, 0, up),
        ay_copy(5, p_up, 1, down),
    ]
    for k in range(4):
        ay[k].start()
    own_copy(c).start()
    for k in range(6):
        ay_copy(k, *arrivals[k], up).wait_recv()
        if k < 2:
            ay[4 + k].start()
        ac_copy(k, c).start()
    for k in range(6):
        ac_copy(k, 1 - c).wait_recv()
        pending.append(ay[k].wait_send)
        pending.append(ac_copy(k, c).wait_send)
    own_copy(1 - c).wait_recv()
    pending.append(own_copy(c).wait_send)

    def block(b):
        return full[b // 3, (b % 3) * BLK : (b % 3 + 1) * BLK, :]

    eye = lax.broadcasted_iota(jnp.int32, (BLK, BLK), 0) == lax.broadcasted_iota(jnp.int32, (BLK, BLK), 1)
    on_diagonal = jnp.where(eye, block(0) + block(3) + block(5), 0.0)
    square_sum = jnp.sum(jnp.sum(on_diagonal, axis=1, keepdims=True), axis=0, keepdims=True)
    factor = 1.0 / (jnp.sqrt(square_sum) + norm_epsilon)
    scale = factor * factor

    def put(stack, p, q, value):
        vh, vl = split(value)
        columns = slice(q * BLK, (q + 1) * BLK)
        for k, v in enumerate((vh, vl, vh)):
            stack[k * FF + p * BLK : k * FF + (p + 1) * BLK, columns] = v

    def put_both(stack, p, q, value):
        put(stack, p, q, value)
        if p != q:
            put(stack, q, p, value.T)

    def panels(stack):
        out = []
        for p in range(3):
            vh = stack[p * BLK : (p + 1) * BLK, :]
            vl = stack[FF + p * BLK : FF + (p + 1) * BLK, :]
            out.append(jnp.concatenate([vh, vh, vl], axis=1))
        return out

    def times(value, stack):
        vh, vl = split(value)
        return dot(jnp.concatenate([vh, vh, vl], axis=1), stack[...])

    for b, (p, q) in enumerate(PAIRS):
        put_both(s_stack, p, q, block(b) * scale)
    s_panels = panels(s_stack)
    for b, (p, q) in enumerate(PAIRS):
        square = dot(s_panels[p], s_stack[:, q * BLK : (q + 1) * BLK])
        value = (second_coeff * scale) * block(b) + third_coeff * square
        if p == q:
            value = value + jnp.where(eye, first_coeff, 0.0)
        put_both(q_stack, p, q, value)

    for b, (p, q) in enumerate(PAIRS):
        put_both(r_stack, p, q, dot(s_panels[p], q_stack[:, q * BLK : (q + 1) * BLK]))
    r_panels = panels(r_stack)
    for b, (p, q) in enumerate(PAIRS):
        put_both(t_stack, p, q, dot(r_panels[p], q_stack[:, q * BLK : (q + 1) * BLK]))
    x1 = times(x0, q_stack) * factor
    t1 = times(x1, t_stack)
    t2 = times(t1, t_stack)
    final = D**0.5 * (first_coeff * x1 + second_coeff * t1 + third_coeff * t2)
    result[...] = final.reshape(NZ, ROWS, FF)

    def ret_copy(s, slot):
        return remote(result.at[s], upd.at[slot], ret_ss.at[s], ret_rs.at[slot], z_peer(s))

    @pl.when(straight)
    def _():
        upd[z] = result[z]

    pl.when(jnp.logical_not(straight))(ret_copy(z, z).start)
    for k in [8, 7, 9, 6, 10, 5, 11, 4, 12, 3, 13, 2, 14, 1, 15]:
        ret_copy((z + k) % NZ, z).start()

    finish()
    for s in range(NZ):
        unless_here(s, ret_copy(s, s).wait_send)
        unless_here(s, ret_copy(s, s).wait_recv)


def shards(gradient, momentum):
    vmem = pl.BlockSpec(memory_space=pltpu.VMEM)
    dma = pltpu.SemaphoreType.DMA
    shape = jax.ShapeDtypeStruct(momentum.shape, f32)
    return pl.pallas_call(
        kernel,
        out_shape=(shape, shape),
        in_specs=[pl.BlockSpec(memory_space=pl.ANY)] * 2,
        out_specs=(vmem, vmem),
        scratch_shapes=[
            pltpu.VMEM(gradient.shape, bf16),
            pltpu.VMEM(momentum.shape, f32),
            pltpu.VMEM((2, WAVES, PER, ROWS, FF), f32),
            pltpu.VMEM((2, WAVES, PER, ROWS, FF), f32),
            pltpu.VMEM((WAVES, PER, ROWS, FF), f32),
            pltpu.VMEM((WAVES, PER, ROWS, FF), f32),
            pltpu.VMEM((NZ, ROWS, FF), f32),
            pltpu.VMEM((6, BLK, BLK), f32),
            pltpu.VMEM((3, BLK, BLK), f32),
            pltpu.VMEM((HALF, BLK), f32),
            pltpu.VMEM((6, HALF_PIECE, BLK), f32),
            pltpu.VMEM((2, HALF_PIECE, BLK), f32),
            pltpu.VMEM((2, HALF, BLK), f32),
            pltpu.VMEM((3 * FF, FF), bf16),
            pltpu.VMEM((3 * FF, FF), bf16),
            pltpu.VMEM((3 * FF, FF), bf16),
            pltpu.VMEM((3 * FF, FF), bf16),
            pltpu.VMEM((NZ, ROWS, FF), f32),
            dma((2, WAVES)),
            dma((2, WAVES)),
            dma((WAVES,)),
            dma((WAVES,)),
            dma((NZ,)),
            dma((NZ,)),
            dma((NZ,)),
            dma((NZ,)),
            dma,
            dma,
            dma((6,)),
            dma((6,)),
            dma((6,)),
            dma((6,)),
            dma((7,)),
            dma((7,)),
            dma((2,)),
            pltpu.SemaphoreType.REGULAR((3,)),
        ],
        compiler_params=pltpu.CompilerParams(
            collective_id=0, has_side_effects=True, vmem_limit_bytes=60 * 2**20
        ),
        name="muon",
    )(gradient, momentum)


def solution(mesh):
    placed = (P("dp", None, "expert", None), P("dp", "expert", None))
    return jax.shard_map(
        shards,
        mesh=mesh,
        in_specs=placed,
        out_specs=(P("dp", "expert", None), P("dp", "expert", None)),
        check_vma=False,
    )
```

```python
import functools

import jax
import jax.numpy as jnp
from jax import lax
from jax.experimental import pallas as pl
from jax.experimental.pallas import tpu as pltpu
from jax.sharding import PartitionSpec as P

D = 2048
FF = 768

first_coeff = 3.4445
second_coeff = -4.775
third_coeff = 2.0315
momentum_keep = 0.95
norm_epsilon = 1e-07

NY, NZ = 4, 16
EXP = 16
ROWS = 16
WAVES = 4
PER = EXP // WAVES
ORDER = (0, 2, 1, 3)
BLK = 256
PAIRS = ((0, 0), (0, 1), (0, 2), (1, 1), (1, 2), (2, 2))
DIAGONAL = (0, 3, 5)
PIECE = BLK // NY
HALF_PIECE = PIECE // 2

PARTS = 2
GC = 1
XAHEAD = 2
MESH = pl.DeviceIdType.MESH
f32 = jnp.float32
bf16 = jnp.bfloat16


def wave_of(i):
    return (i % 2) * 2 + (i // 2) % 2


def split(value):
    high = value.astype(bf16)
    return high, (value - high.astype(f32)).astype(bf16)


def dot(left, right):
    return jnp.dot(left, right, preferred_element_type=f32)


def dot_rows(left, right):
    return lax.dot_general(left, right, (((0,), (0,)), ((), ())), preferred_element_type=f32)


def kernel(
    grad_hbm,
    mom_hbm,
    new_mom,
    upd,
    grad,
    mom,
    core_out,
    core_in,
    x_out,
    x_in,
    rows,
    gram,
    gram_core,
    half,
    ry_in,
    ry_out,
    full,
    s_stack,
    q_stack,
    r_stack,
    t_stack,
    result,
    core_ss,
    core_rs,
    x_ss,
    x_rs,
    fwd_ss,
    fwd_rs,
    ret_ss,
    ret_rs,
    gc_ss,
    gc_rs,
    ry_ss,
    ry_rs,
    ay_ss,
    ay_rs,
    ac_ss,
    ac_rs,
    load_s,
    entered,
    go,
):
    dp = lax.axis_index("dp")
    ex = lax.axis_index("expert")
    h, c = dp // 2, dp % 2
    y, z, a = ex // 32, (ex // 2) % NZ, ex % 2

    other_core = (h * 2 + 1 - c, ex)
    x_partner = ((1 - h) * 2 + c, ex)

    def z_peer(i):
        return (h * 2 + a, y * 32 + i * 2 + c)

    def along_z(d):
        return (dp, y * 32 + ((z + d) % NZ) * 2 + a)

    def y_peer(k):
        return (dp, ((y + k) % NY) * 32 + z * 2 + a)

    def remote(src, dst, ss, rs, to):
        return pltpu.make_async_remote_copy(
            src_ref=src, dst_ref=dst, send_sem=ss, recv_sem=rs, device_id=to, device_id_type=MESH
        )

    straight = a == c

    def base(side, core):
        owner_h = 1 - h if side == 0 else h
        return (owner_h * 2 + core) * EXP

    def grad_load(k):
        quarter = pl.ds(pl.multiple_of(base(k // 2, 1 - c if k % 2 == 0 else c), EXP), EXP)
        return pltpu.make_async_copy(grad_hbm.at[0, quarter], grad.at[0, quarter], load_s.at[k])

    mom_load = pltpu.make_async_copy(mom_hbm, mom, load_s.at[4])
    for k in range(4):
        grad_load(k).start()
    mom_load.start()

    pending = []

    def finish():
        for wait in pending:
            wait()

    def unless_here(s, then):
        pl.when(jnp.logical_not(jnp.logical_and(straight, z == s)))(then)

    barrier = pltpu.get_barrier_semaphore()

    def greet(to):
        pl.semaphore_signal(barrier, inc=1, device_id=to, device_id_type=MESH)

    greet(other_core)
    greet(x_partner)
    for k in range(1, NY):
        greet(y_peer(k))
    for d in (1, NZ - 1):
        greet(along_z(d))

    @pl.when(jnp.logical_not(straight))
    def _():
        for d in (0, 1, NZ - 1):
            greet(z_peer((z + d) % NZ))

    pl.semaphore_wait(barrier, 10 - 3 * straight.astype(jnp.int32))

    def hand_on(step):
        d = 2**step
        for away in (d, NZ - d):
            pl.semaphore_signal(entered.at[step], inc=1, device_id=along_z(away), device_id_type=MESH)

    def heard(step):
        pl.semaphore_wait(entered.at[step], 2)

    def core_copy(side, w):
        return remote(core_out.at[side, w], core_in.at[side, w], core_ss.at[side, w], core_rs.at[side, w], other_core)

    def x_copy(w):
        return remote(x_out.at[w], x_in.at[w], x_ss.at[w], x_rs.at[w], x_partner)

    for side in range(2):
        grad_load(2 * side).wait()
        for w in range(WAVES):
            for j in range(PER):
                core_out[side, w, j] = grad[0, base(side, 1 - c) + WAVES * j + ORDER[w]].astype(f32)
            core_copy(side, w).start()
            pending.append(core_copy(side, w).wait_send)

    def x_send(w):
        core_copy(0, w).wait_recv()
        for j in range(PER):
            x_out[w, j] = grad[0, base(0, c) + WAVES * j + ORDER[w]].astype(f32) + core_in[0, w, j]
        x_copy(w).start()
        pending.append(x_copy(w).wait_send)

    hand_on(0)
    heard(0)
    hand_on(1)
    grad_load(1).wait()
    for w in range(XAHEAD):
        x_send(w)
    heard(1)
    hand_on(2)
    grad_load(3).wait()
    mom_load.wait()

    def fwd_copy(i, slot):
        return remote(new_mom.at[i], rows.at[slot], fwd_ss.at[i], fwd_rs.at[slot], z_peer(i))

    def rows_wait():
        for s in range(NZ):
            unless_here(s, fwd_copy(s, s).wait_recv)

    def tell(i, wave):
        pl.semaphore_signal(go.at[wave], inc=1, device_id=z_peer(i), device_id_type=MESH)

    for w in range(WAVES):
        core_copy(1, w).wait_recv()
        for j in range(PER):
            i = WAVES * j + ORDER[w]
            new_mom[i] = momentum_keep * mom[i] + (grad[0, base(1, c) + i].astype(f32) + core_in[1, w, j])
        x_copy(w).wait_recv()
        if w + XAHEAD < WAVES:
            x_send(w + XAHEAD)
        for j in range(PER):
            i = WAVES * j + ORDER[w]
            new_mom[i] = new_mom[i] + x_in[w, j]
        if w == 1:

            @pl.when(wave_of(z) >= GC)
            def _():
                for j in range(PER):
                    i = WAVES * j + ORDER[0]
                    unless_here(i, fwd_copy(i, i).wait_send)

        if w >= 2:
            done = w - 2

            @pl.when(wave_of(z) == done)
            def _():
                rows_wait()
                for i in range(NZ):
                    if wave_of(i) > done:
                        unless_here(i, functools.partial(tell, i, done))

            @pl.when(wave_of(z) > done)
            def _():
                pl.semaphore_wait(go.at[done], PER)

        for j in range(PER):
            i = WAVES * j + ORDER[w]

            @pl.when(jnp.logical_and(straight, z == i))
            def _():
                rows[i] = new_mom[i]

        if w > 0:
            for j in range(PER):
                i = WAVES * j + ORDER[w]
                unless_here(i, fwd_copy(i, z).start)
        else:
            for j in range(PER):
                i = WAVES * j + ORDER[w]
                pl.when((i - z + 4 + NZ) % NZ <= 8)(functools.partial(unless_here, i, fwd_copy(i, z).start))
            heard(2)
            for j in range(PER):
                i = WAVES * j + ORDER[w]
                pl.when((i - z + 4 + NZ) % NZ > 8)(fwd_copy(i, z).start)

    def fwd_finish():
        for w in range(WAVES):

            def left():
                for j in range(PER):
                    i = WAVES * j + ORDER[w]
                    unless_here(i, fwd_copy(i, i).wait_send)

            if w == 0:
                pl.when(wave_of(z) < GC)(left)
            else:
                left()

    pending.append(fwd_finish)

    pl.when(wave_of(z) >= 2)(rows_wait)

    x0 = rows[...].reshape(NZ * ROWS, FF)
    x_hi, x_lo = split(x0)
    left = jnp.concatenate([x_hi, x_hi, x_lo], axis=0)
    right = jnp.concatenate([x_hi, x_lo, x_hi], axis=0)
    for b, (p, q) in enumerate(PAIRS):
        gram[b] = dot_rows(left[:, p * BLK : (p + 1) * BLK], right[:, q * BLK : (q + 1) * BLK])

    up, down = y_peer(1), y_peer(NY - 1)
    p_up, p_far, p_down = (y + 1) % NY, (y + 2) % NY, (y + NY - 1) % NY

    def part(p, side):
        return pl.ds(pl.multiple_of(p * PIECE + side * HALF_PIECE, HALF_PIECE), HALF_PIECE)

    def gc_copy(k):
        return remote(gram.at[3 * (1 - c) + k], gram_core.at[k], gc_ss.at[k], gc_rs.at[k], other_core)

    def ry_copy(k, n, src, to):
        return remote(src, ry_in.at[k, n], ry_ss.at[k, n], ry_rs.at[k, n], to)

    ry = [
        [
            ry_copy(k, 0, half.at[k, part(p_far, 0)], up),
            ry_copy(k, 1, half.at[k, part(p_far, 1)], down),
            ry_copy(k, 2, half.at[k, part(p_up, 1)], up),
            ry_copy(k, 3, half.at[k, part(p_down, 0)], down),
            ry_copy(k, 4, ry_out.at[k, 0], up),
            ry_copy(k, 5, ry_out.at[k, 1], down),
        ]
        for k in range(3)
    ]

    def ay_copy(k, n, p, side, to):
        place = full.at[c, k, part(p, side)]
        return remote(place, place, ay_ss.at[k, n], ay_rs.at[k, n], to)

    arrivals = ((p_down, 0), (p_up, 1), (p_down, 1), (p_up, 0), (p_far, 0), (p_far, 1))

    def ac_copy(k, n, core):
        place = full.at[core, k, part(*arrivals[n])]
        return remote(place, place, ac_ss.at[k, n], ac_rs.at[k, n], other_core)

    def own_copy(k, core):
        place = full.at[core, k, pl.ds(pl.multiple_of(y * PIECE, PIECE), PIECE)]
        return remote(place, place, ac_ss.at[k, 6], ac_rs.at[k, 6], other_core)

    ay = [
        [
            ay_copy(k, 0, y, 0, up),
            ay_copy(k, 1, y, 1, down),
            ay_copy(k, 2, y, 1, up),
            ay_copy(k, 3, y, 0, down),
            ay_copy(k, 4, p_down, 0, up),
            ay_copy(k, 5, p_up, 1, down),
        ]
        for k in range(3)
    ]

    for k in range(3):
        gc_copy(k).start()
    for k in range(3):
        gc_copy(k).wait_recv()
        half[k] = gram[3 * c + k] + gram_core[k]
        for n in range(4):
            ry[k][n].start()
    for k in range(3):
        for n, p in ((0, p_up), (1, p_down)):
            ry[k][n].wait_recv()
            ry_out[k, n] = ry_in[k, n] + half[k, part(p, n)]
            ry[k][4 + n].start()
    for k in range(3):
        for n in range(2, 6):
            ry[k][n].wait_recv()
        full[c, k, part(y, 0)] = half[k, part(y, 0)] + (ry_in[k, 3] + ry_in[k, 4])
        full[c, k, part(y, 1)] = half[k, part(y, 1)] + (ry_in[k, 2] + ry_in[k, 5])
        for n in range(4):
            ay[k][n].start()
        own_copy(k, c).start()
    for k in range(3):
        for n in range(2):
            ay_copy(k, n, *arrivals[n], up).wait_recv()
            ay[k][4 + n].start()
            ac_copy(k, n, c).start()
    for k in range(3):
        for n in range(2, 6):
            ay_copy(k, n, *arrivals[n], up).wait_recv()
            ac_copy(k, n, c).start()
    for k in range(3):
        own_copy(k, 1 - c).wait_recv()
        pending.append(own_copy(k, c).wait_send)
        pending.append(gc_copy(k).wait_send)
        for n in range(6):
            ac_copy(k, n, 1 - c).wait_recv()
            pending.append(ry[k][n].wait_send)
            pending.append(ay[k][n].wait_send)
            pending.append(ac_copy(k, n, c).wait_send)

    def block(b):
        return full[b // 3, b % 3]

    eye = lax.broadcasted_iota(jnp.int32, (BLK, BLK), 0) == lax.broadcasted_iota(jnp.int32, (BLK, BLK), 1)
    on_diagonal = jnp.where(eye, block(0) + block(3) + block(5), 0.0)
    square_sum = jnp.sum(jnp.sum(on_diagonal, axis=1, keepdims=True), axis=0, keepdims=True)
    factor = 1.0 / (jnp.sqrt(square_sum) + norm_epsilon)
    scale = factor * factor

    def put(stack, p, q, value):
        vh, vl = split(value)
        columns = slice(q * BLK, (q + 1) * BLK)
        for k, v in enumerate((vh, vl, vh)):
            stack[k * FF + p * BLK : k * FF + (p + 1) * BLK, columns] = v

    def put_both(stack, p, q, value):
        put(stack, p, q, value)
        if p != q:
            put(stack, q, p, value.T)

    def panels(stack):
        out = []
        for p in range(3):
            vh = stack[p * BLK : (p + 1) * BLK, :]
            vl = stack[FF + p * BLK : FF + (p + 1) * BLK, :]
            out.append(jnp.concatenate([vh, vh, vl], axis=1))
        return out

    def times(value, stack):
        vh, vl = split(value)
        return dot(jnp.concatenate([vh, vh, vl], axis=1), stack[...])

    for b, (p, q) in enumerate(PAIRS):
        put_both(s_stack, p, q, block(b) * scale)
    s_panels = panels(s_stack)
    for b, (p, q) in enumerate(PAIRS):
        square = dot(s_panels[p], s_stack[:, q * BLK : (q + 1) * BLK])
        value = (second_coeff * scale) * block(b) + third_coeff * square
        if p == q:
            value = value + jnp.where(eye, first_coeff, 0.0)
        put_both(q_stack, p, q, value)

    for b, (p, q) in enumerate(PAIRS):
        put_both(r_stack, p, q, dot(s_panels[p], q_stack[:, q * BLK : (q + 1) * BLK]))
    r_panels = panels(r_stack)
    for b, (p, q) in enumerate(PAIRS):
        put_both(t_stack, p, q, dot(r_panels[p], q_stack[:, q * BLK : (q + 1) * BLK]))

    def ret_copy(s, slot):
        return remote(result.at[s], upd.at[slot], ret_ss.at[s], ret_rs.at[slot], z_peer(s))

    for first in range(0, NZ, NZ // PARTS):
        slots = range(first, first + NZ // PARTS)
        x1 = times(x0[first * ROWS : (first + NZ // PARTS) * ROWS], q_stack) * factor
        t1 = times(x1, t_stack)
        t2 = times(t1, t_stack)
        final = D**0.5 * (first_coeff * x1 + second_coeff * t1 + third_coeff * t2)
        result[first : first + NZ // PARTS] = final.reshape(NZ // PARTS, ROWS, FF)
        for s in slots:

            @pl.when(jnp.logical_and(straight, z == s))
            def _():
                upd[s] = result[s]

            unless_here(s, ret_copy(s, z).start)

    finish()
    for s in range(NZ):
        unless_here(s, ret_copy(s, s).wait_send)
        unless_here(s, ret_copy(s, s).wait_recv)


def shards(gradient, momentum):
    vmem = pl.BlockSpec(memory_space=pltpu.VMEM)
    dma = pltpu.SemaphoreType.DMA
    shape = jax.ShapeDtypeStruct(momentum.shape, f32)
    return pl.pallas_call(
        kernel,
        out_shape=(shape, shape),
        in_specs=[pl.BlockSpec(memory_space=pl.ANY)] * 2,
        out_specs=(vmem, vmem),
        scratch_shapes=[
            pltpu.VMEM(gradient.shape, bf16),
            pltpu.VMEM(momentum.shape, f32),
            pltpu.VMEM((2, WAVES, PER, ROWS, FF), f32),
            pltpu.VMEM((2, WAVES, PER, ROWS, FF), f32),
            pltpu.VMEM((WAVES, PER, ROWS, FF), f32),
            pltpu.VMEM((WAVES, PER, ROWS, FF), f32),
            pltpu.VMEM((NZ, ROWS, FF), f32),
            pltpu.VMEM((6, BLK, BLK), f32),
            pltpu.VMEM((3, BLK, BLK), f32),
            pltpu.VMEM((3, BLK, BLK), f32),
            pltpu.VMEM((3, 6, HALF_PIECE, BLK), f32),
            pltpu.VMEM((3, 2, HALF_PIECE, BLK), f32),
            pltpu.VMEM((2, 3, BLK, BLK), f32),
            pltpu.VMEM((3 * FF, FF), bf16),
            pltpu.VMEM((3 * FF, FF), bf16),
            pltpu.VMEM((3 * FF, FF), bf16),
            pltpu.VMEM((3 * FF, FF), bf16),
            pltpu.VMEM((NZ, ROWS, FF), f32),
            dma((2, WAVES)),
            dma((2, WAVES)),
            dma((WAVES,)),
            dma((WAVES,)),
            dma((NZ,)),
            dma((NZ,)),
            dma((NZ,)),
            dma((NZ,)),
            dma((3,)),
            dma((3,)),
            dma((3, 6)),
            dma((3, 6)),
            dma((3, 6)),
            dma((3, 6)),
            dma((3, 7)),
            dma((3, 7)),
            dma((5,)),
            pltpu.SemaphoreType.REGULAR((3,)),
            pltpu.SemaphoreType.REGULAR((WAVES - 2,)),
        ],
        compiler_params=pltpu.CompilerParams(
            collective_id=0, has_side_effects=True, vmem_limit_bytes=52 * 2**20
        ),
        name="muon",
    )(gradient, momentum)


def solution(mesh):
    placed = (P("dp", None, "expert", None), P("dp", "expert", None))
    return jax.shard_map(
        shards,
        mesh=mesh,
        in_specs=placed,
        out_specs=(P("dp", "expert", None), P("dp", "expert", None)),
        check_vma=False,
    )
```

```python
import functools

import jax
import jax.numpy as jnp
from jax import lax
from jax.experimental import pallas as pl
from jax.experimental.pallas import tpu as pltpu
from jax.sharding import PartitionSpec as P

D = 2048
FF = 768

first_coeff = 3.4445
second_coeff = -4.775
third_coeff = 2.0315
momentum_keep = 0.95
norm_epsilon = 1e-07

NY, NZ = 4, 16
EXP = 16
ROWS = 16
WAVES = 4
PER = EXP // WAVES
ORDER = (0, 2, 1, 3)
BLK = 256
PAIRS = ((0, 0), (0, 1), (0, 2), (1, 1), (1, 2), (2, 2))
DIAGONAL = (0, 3, 5)
PIECE = BLK // NY
HALF_PIECE = PIECE // 2

PARTS = 2
GC = 1
XAHEAD = 3
MESH = pl.DeviceIdType.MESH
f32 = jnp.float32
bf16 = jnp.bfloat16


def wave_of(i):
    return (i % 2) * 2 + (i // 2) % 2


def split(value):
    high = value.astype(bf16)
    return high, (value - high.astype(f32)).astype(bf16)


def dot(left, right):
    return jnp.dot(left, right, preferred_element_type=f32)


def dot_rows(left, right):
    return lax.dot_general(left, right, (((0,), (0,)), ((), ())), preferred_element_type=f32)


def kernel(
    grad_hbm,
    mom_hbm,
    new_mom,
    upd,
    grad,
    mom,
    core_out,
    core_in,
    x_out,
    x_in,
    rows,
    gram,
    gram_core,
    half,
    ry_in,
    ry_out,
    full,
    s_stack,
    q_stack,
    r_stack,
    t_stack,
    result,
    core_ss,
    core_rs,
    x_ss,
    x_rs,
    fwd_ss,
    fwd_rs,
    ret_ss,
    ret_rs,
    gc_ss,
    gc_rs,
    ry_ss,
    ry_rs,
    ay_ss,
    ay_rs,
    ac_ss,
    ac_rs,
    load_s,
    entered,
    go,
):
    dp = lax.axis_index("dp")
    ex = lax.axis_index("expert")
    h, c = dp // 2, dp % 2
    y, z, a = ex // 32, (ex // 2) % NZ, ex % 2

    other_core = (h * 2 + 1 - c, ex)
    x_partner = ((1 - h) * 2 + c, ex)

    def z_peer(i):
        return (h * 2 + a, y * 32 + i * 2 + c)

    def along_z(d):
        return (dp, y * 32 + ((z + d) % NZ) * 2 + a)

    def y_peer(k):
        return (dp, ((y + k) % NY) * 32 + z * 2 + a)

    def remote(src, dst, ss, rs, to):
        return pltpu.make_async_remote_copy(
            src_ref=src, dst_ref=dst, send_sem=ss, recv_sem=rs, device_id=to, device_id_type=MESH
        )

    straight = a == c

    def base(side, core):
        owner_h = 1 - h if side == 0 else h
        return (owner_h * 2 + core) * EXP

    def grad_load(k):
        quarter = pl.ds(pl.multiple_of(base(k // 2, 1 - c if k % 2 == 0 else c), EXP), EXP)
        return pltpu.make_async_copy(grad_hbm.at[0, quarter], grad.at[0, quarter], load_s.at[k])

    mom_load = pltpu.make_async_copy(mom_hbm, mom, load_s.at[4])
    for k in range(4):
        grad_load(k).start()
    mom_load.start()

    pending = []

    def finish():
        for wait in pending:
            wait()

    def unless_here(s, then):
        pl.when(jnp.logical_not(jnp.logical_and(straight, z == s)))(then)

    barrier = pltpu.get_barrier_semaphore()

    def greet(to):
        pl.semaphore_signal(barrier, inc=1, device_id=to, device_id_type=MESH)

    greet(other_core)
    greet(x_partner)
    for k in range(1, NY):
        greet(y_peer(k))
    for d in (1, NZ - 1):
        greet(along_z(d))

    @pl.when(jnp.logical_not(straight))
    def _():
        for d in (0, 1, NZ - 1):
            greet(z_peer((z + d) % NZ))

    pl.semaphore_wait(barrier, 10 - 3 * straight.astype(jnp.int32))

    def hand_on(step):
        d = 2**step
        for away in (d, NZ - d):
            pl.semaphore_signal(entered.at[step], inc=1, device_id=along_z(away), device_id_type=MESH)

    def heard(step):
        pl.semaphore_wait(entered.at[step], 2)

    def core_copy(side, w):
        return remote(core_out.at[side, w], core_in.at[side, w], core_ss.at[side, w], core_rs.at[side, w], other_core)

    def x_copy(w):
        return remote(x_out.at[w], x_in.at[w], x_ss.at[w], x_rs.at[w], x_partner)

    for side in range(2):
        grad_load(2 * side).wait()
        for w in range(WAVES):
            for j in range(PER):
                core_out[side, w, j] = grad[0, base(side, 1 - c) + WAVES * j + ORDER[w]].astype(f32)
            core_copy(side, w).start()
            pending.append(core_copy(side, w).wait_send)

    def x_send(w):
        core_copy(0, w).wait_recv()
        for j in range(PER):
            x_out[w, j] = grad[0, base(0, c) + WAVES * j + ORDER[w]].astype(f32) + core_in[0, w, j]
        x_copy(w).start()
        pending.append(x_copy(w).wait_send)

    hand_on(0)
    heard(0)
    hand_on(1)
    grad_load(1).wait()
    for w in range(XAHEAD):
        x_send(w)
    heard(1)
    hand_on(2)
    grad_load(3).wait()
    mom_load.wait()

    def fwd_copy(i, slot):
        return remote(new_mom.at[i], rows.at[slot], fwd_ss.at[i], fwd_rs.at[slot], z_peer(i))

    def rows_wait():
        for s in range(NZ):
            unless_here(s, fwd_copy(s, s).wait_recv)

    def tell(i, wave):
        pl.semaphore_signal(go.at[wave], inc=1, device_id=z_peer(i), device_id_type=MESH)

    for w in range(WAVES):
        core_copy(1, w).wait_recv()
        for j in range(PER):
            i = WAVES * j + ORDER[w]
            new_mom[i] = momentum_keep * mom[i] + (grad[0, base(1, c) + i].astype(f32) + core_in[1, w, j])
        x_copy(w).wait_recv()
        if w + XAHEAD < WAVES:
            x_send(w + XAHEAD)
        for j in range(PER):
            i = WAVES * j + ORDER[w]
            new_mom[i] = new_mom[i] + x_in[w, j]
        if w == 1:

            @pl.when(wave_of(z) >= GC)
            def _():
                for j in range(PER):
                    i = WAVES * j + ORDER[0]
                    unless_here(i, fwd_copy(i, i).wait_send)

        if w >= 2:
            done = w - 2

            @pl.when(wave_of(z) == done)
            def _():
                rows_wait()
                for i in range(NZ):
                    if wave_of(i) > done:
                        unless_here(i, functools.partial(tell, i, done))

            @pl.when(wave_of(z) > done)
            def _():
                pl.semaphore_wait(go.at[done], PER)

        for j in range(PER):
            i = WAVES * j + ORDER[w]

            @pl.when(jnp.logical_and(straight, z == i))
            def _():
                rows[i] = new_mom[i]

        if w > 0:
            for j in range(PER):
                i = WAVES * j + ORDER[w]
                unless_here(i, fwd_copy(i, z).start)
        else:
            for j in range(PER):
                i = WAVES * j + ORDER[w]
                pl.when((i - z + 4 + NZ) % NZ <= 8)(functools.partial(unless_here, i, fwd_copy(i, z).start))
            heard(2)
            for j in range(PER):
                i = WAVES * j + ORDER[w]
                pl.when((i - z + 4 + NZ) % NZ > 8)(fwd_copy(i, z).start)

    def fwd_finish():
        for w in range(WAVES):

            def left():
                for j in range(PER):
                    i = WAVES * j + ORDER[w]
                    unless_here(i, fwd_copy(i, i).wait_send)

            if w == 0:
                pl.when(wave_of(z) < GC)(left)
            else:
                left()

    pending.append(fwd_finish)

    pl.when(wave_of(z) >= 2)(rows_wait)

    x0 = rows[...].reshape(NZ * ROWS, FF)
    x_hi, x_lo = split(x0)
    left = jnp.concatenate([x_hi, x_hi, x_lo], axis=0)
    right = jnp.concatenate([x_hi, x_lo, x_hi], axis=0)
    up, down = y_peer(1), y_peer(NY - 1)
    p_up, p_far, p_down = (y + 1) % NY, (y + 2) % NY, (y + NY - 1) % NY

    def part(p, side):
        return pl.ds(pl.multiple_of(p * PIECE + side * HALF_PIECE, HALF_PIECE), HALF_PIECE)

    def gc_copy(k):
        return remote(gram.at[3 * (1 - c) + k], gram_core.at[k], gc_ss.at[k], gc_rs.at[k], other_core)

    def ry_copy(k, n, src, to):
        return remote(src, ry_in.at[k, n], ry_ss.at[k, n], ry_rs.at[k, n], to)

    ry = [
        [
            ry_copy(k, 0, half.at[k, part(p_far, 0)], up),
            ry_copy(k, 1, half.at[k, part(p_far, 1)], down),
            ry_copy(k, 2, half.at[k, part(p_up, 1)], up),
            ry_copy(k, 3, half.at[k, part(p_down, 0)], down),
            ry_copy(k, 4, ry_out.at[k, 0], up),
            ry_copy(k, 5, ry_out.at[k, 1], down),
        ]
        for k in range(3)
    ]

    def ay_copy(k, n, p, side, to):
        place = full.at[c, k, part(p, side)]
        return remote(place, place, ay_ss.at[k, n], ay_rs.at[k, n], to)

    arrivals = ((p_down, 0), (p_up, 1), (p_down, 1), (p_up, 0), (p_far, 0), (p_far, 1))

    def ac_copy(k, n, core):
        place = full.at[core, k, part(*arrivals[n])]
        return remote(place, place, ac_ss.at[k, n], ac_rs.at[k, n], other_core)

    def own_copy(k, core):
        place = full.at[core, k, pl.ds(pl.multiple_of(y * PIECE, PIECE), PIECE)]
        return remote(place, place, ac_ss.at[k, 6], ac_rs.at[k, 6], other_core)

    ay = [
        [
            ay_copy(k, 0, y, 0, up),
            ay_copy(k, 1, y, 1, down),
            ay_copy(k, 2, y, 1, up),
            ay_copy(k, 3, y, 0, down),
            ay_copy(k, 4, p_down, 0, up),
            ay_copy(k, 5, p_up, 1, down),
        ]
        for k in range(3)
    ]

    for k in range(3):
        for b in (k, 3 + k):
            p, q = PAIRS[b]
            gram[b] = dot_rows(left[:, p * BLK : (p + 1) * BLK], right[:, q * BLK : (q + 1) * BLK])
        gc_copy(k).start()
    for k in range(3):
        gc_copy(k).wait_recv()
        half[k] = gram[3 * c + k] + gram_core[k]
        for n in range(4):
            ry[k][n].start()
    for k in range(3):
        for n, p in ((0, p_up), (1, p_down)):
            ry[k][n].wait_recv()
            ry_out[k, n] = ry_in[k, n] + half[k, part(p, n)]
            ry[k][4 + n].start()
    for k in range(3):
        for n in range(2, 6):
            ry[k][n].wait_recv()
        full[c, k, part(y, 0)] = half[k, part(y, 0)] + (ry_in[k, 3] + ry_in[k, 4])
        full[c, k, part(y, 1)] = half[k, part(y, 1)] + (ry_in[k, 2] + ry_in[k, 5])
        for n in range(4):
            ay[k][n].start()
        own_copy(k, c).start()
    for k in range(3):
        for n in range(2):
            ay_copy(k, n, *arrivals[n], up).wait_recv()
            ay[k][4 + n].start()
            ac_copy(k, n, c).start()
    for k in range(3):
        for n in range(2, 6):
            ay_copy(k, n, *arrivals[n], up).wait_recv()
            ac_copy(k, n, c).start()
    for k in range(3):
        own_copy(k, 1 - c).wait_recv()
        pending.append(own_copy(k, c).wait_send)
        pending.append(gc_copy(k).wait_send)
        for n in range(6):
            ac_copy(k, n, 1 - c).wait_recv()
            pending.append(ry[k][n].wait_send)
            pending.append(ay[k][n].wait_send)
            pending.append(ac_copy(k, n, c).wait_send)

    def block(b):
        return full[b // 3, b % 3]

    eye = lax.broadcasted_iota(jnp.int32, (BLK, BLK), 0) == lax.broadcasted_iota(jnp.int32, (BLK, BLK), 1)
    on_diagonal = jnp.where(eye, block(0) + block(3) + block(5), 0.0)
    square_sum = jnp.sum(jnp.sum(on_diagonal, axis=1, keepdims=True), axis=0, keepdims=True)
    factor = 1.0 / (jnp.sqrt(square_sum) + norm_epsilon)
    scale = factor * factor

    def put(stack, p, q, value):
        vh, vl = split(value)
        columns = slice(q * BLK, (q + 1) * BLK)
        for k, v in enumerate((vh, vl, vh)):
            stack[k * FF + p * BLK : k * FF + (p + 1) * BLK, columns] = v

    def put_both(stack, p, q, value):
        put(stack, p, q, value)
        if p != q:
            put(stack, q, p, value.T)

    def panels(stack):
        out = []
        for p in range(3):
            vh = stack[p * BLK : (p + 1) * BLK, :]
            vl = stack[FF + p * BLK : FF + (p + 1) * BLK, :]
            out.append(jnp.concatenate([vh, vh, vl], axis=1))
        return out

    def times(value, stack):
        vh, vl = split(value)
        return dot(jnp.concatenate([vh, vh, vl], axis=1), stack[...])

    for b, (p, q) in enumerate(PAIRS):
        put_both(s_stack, p, q, block(b) * scale)
    s_panels = panels(s_stack)
    for b, (p, q) in enumerate(PAIRS):
        square = dot(s_panels[p], s_stack[:, q * BLK : (q + 1) * BLK])
        value = (second_coeff * scale) * block(b) + third_coeff * square
        if p == q:
            value = value + jnp.where(eye, first_coeff, 0.0)
        put_both(q_stack, p, q, value)

    for b, (p, q) in enumerate(PAIRS):
        put_both(r_stack, p, q, dot(s_panels[p], q_stack[:, q * BLK : (q + 1) * BLK]))
    r_panels = panels(r_stack)
    for b, (p, q) in enumerate(PAIRS):
        put_both(t_stack, p, q, dot(r_panels[p], q_stack[:, q * BLK : (q + 1) * BLK]))

    def ret_copy(s, slot):
        return remote(result.at[s], upd.at[slot], ret_ss.at[s], ret_rs.at[slot], z_peer(s))

    for first in range(0, NZ, NZ // PARTS):
        slots = range(first, first + NZ // PARTS)
        x1 = times(x0[first * ROWS : (first + NZ // PARTS) * ROWS], q_stack) * factor
        t1 = times(x1, t_stack)
        t2 = times(t1, t_stack)
        final = D**0.5 * (first_coeff * x1 + second_coeff * t1 + third_coeff * t2)
        result[first : first + NZ // PARTS] = final.reshape(NZ // PARTS, ROWS, FF)
        for s in slots:

            @pl.when(jnp.logical_and(straight, z == s))
            def _():
                upd[s] = result[s]

            unless_here(s, ret_copy(s, z).start)

    finish()
    for s in range(NZ):
        unless_here(s, ret_copy(s, s).wait_send)
        unless_here(s, ret_copy(s, s).wait_recv)


def shards(gradient, momentum):
    vmem = pl.BlockSpec(memory_space=pltpu.VMEM)
    dma = pltpu.SemaphoreType.DMA
    shape = jax.ShapeDtypeStruct(momentum.shape, f32)
    return pl.pallas_call(
        kernel,
        out_shape=(shape, shape),
        in_specs=[pl.BlockSpec(memory_space=pl.ANY)] * 2,
        out_specs=(vmem, vmem),
        scratch_shapes=[
            pltpu.VMEM(gradient.shape, bf16),
            pltpu.VMEM(momentum.shape, f32),
            pltpu.VMEM((2, WAVES, PER, ROWS, FF), f32),
            pltpu.VMEM((2, WAVES, PER, ROWS, FF), f32),
            pltpu.VMEM((WAVES, PER, ROWS, FF), f32),
            pltpu.VMEM((WAVES, PER, ROWS, FF), f32),
            pltpu.VMEM((NZ, ROWS, FF), f32),
            pltpu.VMEM((6, BLK, BLK), f32),
            pltpu.VMEM((3, BLK, BLK), f32),
            pltpu.VMEM((3, BLK, BLK), f32),
            pltpu.VMEM((3, 6, HALF_PIECE, BLK), f32),
            pltpu.VMEM((3, 2, HALF_PIECE, BLK), f32),
            pltpu.VMEM((2, 3, BLK, BLK), f32),
            pltpu.VMEM((3 * FF, FF), bf16),
            pltpu.VMEM((3 * FF, FF), bf16),
            pltpu.VMEM((3 * FF, FF), bf16),
            pltpu.VMEM((3 * FF, FF), bf16),
            pltpu.VMEM((NZ, ROWS, FF), f32),
            dma((2, WAVES)),
            dma((2, WAVES)),
            dma((WAVES,)),
            dma((WAVES,)),
            dma((NZ,)),
            dma((NZ,)),
            dma((NZ,)),
            dma((NZ,)),
            dma((3,)),
            dma((3,)),
            dma((3, 6)),
            dma((3, 6)),
            dma((3, 6)),
            dma((3, 6)),
            dma((3, 7)),
            dma((3, 7)),
            dma((5,)),
            pltpu.SemaphoreType.REGULAR((3,)),
            pltpu.SemaphoreType.REGULAR((WAVES - 2,)),
        ],
        compiler_params=pltpu.CompilerParams(
            collective_id=0, has_side_effects=True, vmem_limit_bytes=52 * 2**20
        ),
        name="muon",
    )(gradient, momentum)


def solution(mesh):
    placed = (P("dp", None, "expert", None), P("dp", "expert", None))
    return jax.shard_map(
        shards,
        mesh=mesh,
        in_specs=placed,
        out_specs=(P("dp", "expert", None), P("dp", "expert", None)),
        check_vma=False,
    )
```
